256 devices in a mesh: blk: 32 (over z, y_lo, core), seq: 8 (over x, y_hi).
Axes of the slice: x: 4, y: 4 (y_hi: 2, y_lo: 2; y = y_hi * 2 + y_lo), z: 8, core: 2. Of those that a mesh axis runs over, the one named last changes fastest.
Arguments:
- tokens: bfloat16 [32, 1024, 4096], P('blk', 'seq'), may hold values from -6 to 6
- norm_gain: bfloat16 [4096], replicated, may hold values from 0.099609375 to 1.8984375
- query_weight: bfloat16 [4096, 4096], P('blk', 'seq')
- key_weight: bfloat16 [4096, 1024], P('blk', 'seq')
- value_weight: bfloat16 [4096, 1024], P('blk', 'seq'), may hold values from -0.09375 to 0.09375
- segment_ids: int32 [32, 1024], P('blk'), may hold values from 0 to 3, never falling along the last dimension, each value on 1 to 512 neighbouring positions
- out_cotangent: bfloat16 [32, 1024, 4096], P('blk', 'seq'), may hold values from -0.119628906 to 0.119628906
Outputs:
- head_mix: bfloat16 [32, 1024, 4096], P('blk', 'seq')
- grad_output_proj: float32 [4096, 4096], P('blk', 'seq')
The draws below stay inside these ranges and needn't reach their ends.
Inputs may be any that keep to these rules, and one draw needn't show every extreme that they name: `segment_ids`: within each sequence the ids never fall, each document is at most 512 tokens long and one is exactly that long.
All inputs are finite; a program needn't handle non-finite values.
Results may differ from the reference program's by a relative error of at most 0.03.
Values may be sent and summed in bfloat16 or wider, within the bound.
No kernel may reach another device: no remote copies, remote signals or barrier semaphores. Data moves between devices by JAX's collectives and lax.ppermute only.
A program may use at most 128 MiB of HBM per device.

```python
import math
import jax
import jax.numpy as jnp
import numpy as np
from jax import lax

D = 4096
HEADS = 32
KV_HEADS = 8
HEAD_DIM = 128
SEGS = 4
SEQ = 1024
MICRO = 32


def shared_query(key):
    return jax.random.normal(key, (D, D), jnp.float32) * D ** (-0.5)


def draw_query_weight(key, part):
    return shared_query(key).astype(jnp.bfloat16)


def draw_key_weight(key, part):
    key = jax.random.fold_in(key, 11)
    own = jax.random.normal(key, (D, KV_HEADS * HEAD_DIM), jnp.float32) * D ** (-0.5)
    return own.astype(jnp.bfloat16)


def spiked(drawn, own_key, source, target, shards_of, factor):
    owner, partner = [(jnp.arange(drawn.shape[dim]) // (drawn.shape[dim] // shards_of)).reshape([-1 if axis == dim else 1 for axis in range(drawn.ndim)]) for dim in (source, target)]
    chosen = jax.random.permutation(own_key, shards_of)[partner]
    strong = (owner == chosen) | (owner == (partner + shards_of // 2) % shards_of)
    return jnp.where(strong, factor * drawn, drawn)


def level_of(rng, shape, split, smallest, high):
    def one(position, parts):
        draws = jax.random.uniform(jax.random.fold_in(jax.random.fold_in(rng, 6), position), (parts,), jnp.float32, smallest / len(split), high / len(split))
        return jnp.repeat(jnp.exp(draws), shape[position] // parts).reshape((-1,) + (1,) * (len(shape) - position - 1))

    level = one(*split[0])
    for cut in split[1:]:
        level = level * one(*cut)
    return level


def length_profile(amount, total, bound, lean):
    portions = [(1 << 20) // math.isqrt(rank ** lean) + 1 for rank in range(2, amount + 1)]
    spare, given = total - bound - (amount - 1), [1] * (amount - 1)
    while spare > 0:
        candidates = [i for i in range(amount - 1) if given[i] < bound]
        whole, left = sum([portions[i] for i in candidates]), spare
        for i in candidates:
            more = min(bound - given[i], max(1, left * portions[i] // whole), spare)
            given[i] = given[i] + more
            spare = spare - more
    return np.array([bound] + given)


def uneven(key, number_of, total, reach, lean):
    if number_of == 2:
        one = jax.random.randint(key, (), max(1, total - reach), min(reach, total - 1) + 1)
        return jnp.stack([one, total - one])
    tallies = jnp.asarray(length_profile(number_of, total, reach, lean), jnp.int32)
    twos = (number_of - 1) // 2
    source_of, sink = tallies[1:1 + 2 * twos:2], tallies[2:2 + 2 * twos:2]
    margin = jnp.minimum(source_of - 1, reach - sink)
    moved = jax.random.randint(jax.random.fold_in(key, 1), (twos,), 0, 1 << 20) % (margin + 1)
    tallies = tallies.at[1:1 + 2 * twos:2].set(source_of - moved).at[2:2 + 2 * twos:2].set(sink + moved)
    return tallies[jax.random.permutation(jax.random.fold_in(key, 2), number_of)]


def normal_values(key, shape, spread, most, split=(), held_as=jnp.bfloat16):
    drawn = spread * jax.random.normal(key, shape, jnp.float32)
    if split:
        drawn = drawn * level_of(key, shape, split, -0.22, 0.18)
    return jnp.clip(drawn, -most, most).astype(held_as)


def heavy_noise(stream_key, shape, width, limit, pieces, heavy, kind=jnp.bfloat16):
    drawn = width * jax.random.normal(stream_key, shape, jnp.float32)
    if pieces:
        drawn = drawn * level_of(stream_key, shape, pieces, -0.22, 0.18)
    return jnp.clip(spiked(drawn, jax.random.fold_in(stream_key, 3), *heavy), -limit, limit).astype(kind)


def setup_inputs(seed: int = 0) -> dict:
    key_list = jax.random.split(jax.random.key(seed), 8)
    tokens = normal_values(key_list[0], (MICRO, SEQ, D), 1.0, 6.0, ((0, 32), (1, 8)))
    norm_gain = jnp.clip(1.0 + 0.18 * jax.random.normal(key_list[1], (D,), jnp.float32), 0.099609375, 1.8984375).astype(jnp.bfloat16)
    query_weight = draw_query_weight(jax.random.fold_in(key_list[7], 71), 0)
    key_weight = draw_key_weight(jax.random.fold_in(key_list[7], 71), 0)
    value_weight = normal_values(key_list[4], (D, KV_HEADS * HEAD_DIM), D ** -0.5, 0.09375, ((0, 32), (1, 8)))
    segment_ids = jax.vmap(lambda own: jnp.searchsorted(jnp.cumsum(uneven(own, SEGS, SEQ, SEQ // 2, 0)), jnp.arange(SEQ), side="right"))(jax.random.split(key_list[5], MICRO)).reshape((MICRO, SEQ)).astype(jnp.int32)
    out_cotangent = heavy_noise(key_list[6], (MICRO, SEQ, D), 0.02, 0.119628906, ((0, 32), (1, 8)), (0, 2, 32, 2.75))
    return {"tokens": tokens, "norm_gain": norm_gain, "query_weight": query_weight, "key_weight": key_weight, "value_weight": value_weight, "segment_ids": segment_ids, "out_cotangent": out_cotangent}


def normed_rows(rows, gain):
    values = rows.astype(jnp.float32)
    meansq = lax.optimization_barrier(jnp.mean(values * values, axis=-1, keepdims=True))
    return (values * lax.rsqrt(meansq + 1e-05) * gain.astype(jnp.float32)).astype(jnp.bfloat16)

def rotate(heads, positions):
    half = heads.shape[-1] // 2
    expo = jnp.arange(half, dtype=jnp.float32) * (2.0 / heads.shape[-1])
    freq = jnp.power(jnp.float32(500000.0), -expo)
    angle = positions.astype(jnp.float32)[:, None] * freq[None, :]
    cosine = jnp.cos(angle)[:, None, :]
    sine = jnp.sin(angle)[:, None, :]
    first = heads[..., :half]
    second = heads[..., half:]
    return jnp.concatenate([first * cosine - second * sine, second * cosine + first * sine], axis=-1)

def attend(grouped, keys, values, segment, start):
    block = grouped.shape[0]
    seq_len = keys.shape[0]
    scores = jnp.einsum('qkgd,skd->kgqs', grouped.astype(jnp.float32), keys.astype(jnp.float32)) * HEAD_DIM ** (-0.5)
    query_pos = start + jnp.arange(block, dtype=jnp.int32)
    key_pos = jnp.arange(seq_len, dtype=jnp.int32)
    query_seg = lax.dynamic_slice_in_dim(segment, start, block, 0)
    allowed = (key_pos[None, :] <= query_pos[:, None]) & (segment[None, :] == query_seg[:, None])
    kept = jnp.where(allowed[None, None], scores, -jnp.inf)
    highest = lax.optimization_barrier(jnp.max(kept, axis=-1, keepdims=True))
    expd = jnp.exp(kept - highest)
    weights = (expd / lax.optimization_barrier(jnp.sum(expd, axis=-1, keepdims=True))).astype(jnp.bfloat16)
    mixed = jnp.einsum('kgqs,skd->qkgd', weights.astype(jnp.float32), values.astype(jnp.float32))
    return mixed.astype(jnp.bfloat16).reshape(block, -1)

def one_sequence(rows, segment, gain, query_weight, key_weight, value_weight):
    seq_len = rows.shape[0]
    normed = normed_rows(rows, gain)
    positions = jnp.arange(seq_len, dtype=jnp.int32)
    query_sum = jnp.dot(normed, query_weight, preferred_element_type=jnp.float32)
    key_sum = jnp.dot(normed, key_weight, preferred_element_type=jnp.float32)
    value_sum = jnp.dot(normed, value_weight, preferred_element_type=jnp.float32)
    queries = rotate(query_sum.reshape(seq_len, HEADS, HEAD_DIM), positions).astype(jnp.bfloat16)
    keys = rotate(key_sum.reshape(seq_len, KV_HEADS, HEAD_DIM), positions).astype(jnp.bfloat16)
    values = value_sum.astype(jnp.bfloat16).reshape(seq_len, KV_HEADS, HEAD_DIM)
    grouped = queries.reshape(seq_len, KV_HEADS, HEADS // KV_HEADS, HEAD_DIM)
    block = min(512, seq_len)

    def one_block(index):
        start = (index * block).astype(jnp.int32)
        piece = lax.dynamic_slice_in_dim(grouped, start, block, 0)
        return attend(piece, keys, values, segment, start)
    blocks = lax.map(one_block, jnp.arange(seq_len // block, dtype=jnp.int32))
    return blocks.reshape(seq_len, HEADS * HEAD_DIM)

def reference(tokens, norm_gain, query_weight, key_weight, value_weight, segment_ids, out_cotangent):

    def per_batch(pair):
        return one_sequence(pair[0], pair[1], norm_gain, query_weight, key_weight, value_weight)
    head_mix = lax.map(per_batch, (tokens, segment_ids))

    def accumulate(total, pair):
        term = lax.dot_general(pair[0], pair[1], (((0,), (0,)), ((), ())), preferred_element_type=jnp.float32)
        return (total + term, None)
    start_total = jnp.zeros((out_cotangent.shape[2], head_mix.shape[2]), jnp.float32)
    grad_output_proj, unused = lax.scan(accumulate, start_total, (out_cotangent, head_mix))
    return (head_mix, grad_output_proj)
```

```python
import functools
import math

import jax
import jax.numpy as jnp
from jax import lax
from jax.experimental import pallas as pl
from jax.experimental.pallas import tpu as pltpu
from jax.sharding import PartitionSpec as P

HEAD_DIM = 128
LANE = 128
NX, NY, NZ = 4, 4, 8
STEPS_Z = (0, -1, 1, -2, 2, -3, 3, 4)
STEPS_X = (0, -1, 1, 2)
F32 = jnp.float32
BF16 = jnp.bfloat16


def move(value, target):
    pairs = []
    for blk in range(32):
        for seq in range(8):
            z, lo, core = blk // 4, (blk // 2) % 2, blk % 2
            x, hi = seq // 2, seq % 2
            tx, ty, tz, tc = target(x, hi * 2 + lo, z, core)
            tx, ty, tz = tx % NX, ty % NY, tz % NZ
            pairs.append((blk * 8 + seq, (tz * 4 + (ty % 2) * 2 + tc) * 8 + tx * 2 + ty // 2))
    return lax.ppermute(value, ("blk", "seq"), pairs)


def to_x(step):
    return lambda x, y, z, c: (x + step, y, z, c)


def to_y(flip):
    return lambda x, y, z, c: (x, y ^ flip, z, c)


def to_z(step):
    return lambda x, y, z, c: (x, y, z + step, c)


def to_core(x, y, z, c):
    return (x, y, z, 1 - c)


def prepare_kernel(order_ref, tok_ref, gain_ref, cot_ref, normed_ref, cot_out_ref):
    values = tok_ref[...].astype(F32)
    inverse = lax.rsqrt(jnp.mean(values * values, axis=-1, keepdims=True) + 1e-05)
    for j in range(32):
        src = pl.ds(pl.multiple_of(order_ref[0, j] * LANE, LANE), LANE)
        dst = pl.ds(j * LANE, LANE)
        part = tok_ref[:, src].astype(F32) * inverse * gain_ref[:, src].astype(F32)
        normed_ref[:, dst] = part.astype(BF16)
        src = pl.ds(pl.multiple_of(order_ref[1, j] * LANE, LANE), LANE)
        cot_out_ref[:, dst] = cot_ref[:, src]


def prepare(order, tokens, gain, cot):
    shape = jax.ShapeDtypeStruct(tokens.shape, BF16)
    full = pl.BlockSpec(memory_space=pltpu.VMEM)
    return pl.pallas_call(
        prepare_kernel,
        in_specs=[pl.BlockSpec(memory_space=pltpu.SMEM), full, full, full],
        out_specs=[full, full],
        out_shape=[shape, shape],
        name="norm_and_order",
    )(order, tokens, gain.reshape(1, -1), cot)


def turned(values, cosine, sine):
    return values * cosine + pltpu.roll(values, HEAD_DIM // 2, 1) * sine


def pack_kernel(a_ref, b_ref, c_ref, d_ref, out_ref):
    for i, ref in enumerate((a_ref, b_ref, c_ref, d_ref)):
        out_ref[(i // 2) * LANE : (i // 2 + 1) * LANE, (i % 2) * 512 : (i % 2 + 1) * 512] = ref[...]


def pack_queries(parts):
    full = pl.BlockSpec(memory_space=pltpu.VMEM)
    return pl.pallas_call(
        pack_kernel,
        in_specs=[full] * 4,
        out_specs=full,
        out_shape=jax.ShapeDtypeStruct((256, 1024), BF16),
        name="pack_queries",
    )(*parts)


def all_z_and_cores(block):
    groups = [[z * 4 + lo * 2 + core for z in range(8) for core in range(2)] for lo in range(2)]
    return lax.all_gather(block, "blk", axis=0, tiled=True, axis_index_groups=groups)


def stack_kernel(where_ref, *refs):
    out_ref = refs[-1]
    for i, ref in enumerate(refs[:7]):
        out_ref[pl.ds(pl.multiple_of(where_ref[i] * LANE, LANE), LANE), :] = ref[...]
    for half in range(2):
        dst = pl.ds(pl.multiple_of(where_ref[7] * LANE + half * 64, 64), 64)
        out_ref[dst, :] = refs[7 + half][...]


def stack_z(where, parts):
    full = pl.BlockSpec(memory_space=pltpu.VMEM)
    return pl.pallas_call(
        stack_kernel,
        in_specs=[pl.BlockSpec(memory_space=pltpu.SMEM)] + [full] * 9,
        out_specs=full,
        out_shape=jax.ShapeDtypeStruct((1024, 256), BF16),
        name="stack_z",
    )(where, *parts)


def kv_kernel(core_ref, x_ref, *refs):
    pieces, (cos_ref, sin_ref, out_ref, weight_ref) = refs[:8], refs[8:]
    for i, ref in enumerate(pieces):
        core = core_ref[0] if i < 4 else 1 - core_ref[0]
        lo, hi = (i % 4) // 2, i % 2

        @pl.loop(0, NZ)
        def _(z, ref=ref, core=core, lo=lo, hi=hi):
            src = pl.ds(pl.multiple_of(z * LANE, LANE), LANE)
            dst = pl.ds(pl.multiple_of(z * 512 + core * 256 + lo * LANE, LANE), LANE)
            weight_ref[dst, hi * LANE : (hi + 1) * LANE] = ref[src, :LANE]
            weight_ref[dst, (2 + hi) * LANE : (3 + hi) * LANE] = ref[src, LANE:]

    total = jnp.dot(x_ref[...], weight_ref[...], preferred_element_type=F32)
    for h in range(2):
        cols = slice(h * LANE, (h + 1) * LANE)
        out_ref[:, cols] = turned(total[:, cols], cos_ref[...], sin_ref[...]).astype(BF16)
    out_ref[:, 2 * LANE :] = total[:, 2 * LANE :].astype(BF16)


def keys_values(core, normed, pieces, cosine, sine):
    full = pl.BlockSpec(memory_space=pltpu.VMEM)
    return pl.pallas_call(
        kv_kernel,
        in_specs=[pl.BlockSpec(memory_space=pltpu.SMEM)] + [full] * 11,
        out_specs=full,
        out_shape=jax.ShapeDtypeStruct((512, 512), BF16),
        scratch_shapes=[pltpu.VMEM((4096, 512), BF16)],
        compiler_params=pltpu.CompilerParams(vmem_limit_bytes=40 * 2**20),
        name="keys_values",
    )(core.reshape(1), normed, *pieces, cosine, sine)


def attend_kernel(chunk_ref, q_ref, own_ref, other_ref, cos_ref, sin_ref, start_ref, out_ref, kv_ref):
    j = pl.program_id(0)

    @pl.when(j == 0)
    def _():
        for i in range(4):
            rows = slice(i * LANE, (i + 1) * LANE)
            chunk = chunk_ref[i]
            there = chunk_ref[4 + i]
            kv_ref[pl.ds(pl.multiple_of(chunk * LANE, LANE), LANE), :] = own_ref[rows, :]
            dest = pl.ds(pl.multiple_of(there * LANE, LANE), LANE)
            for a, b in ((0, 1), (1, 0), (2, 3), (3, 2)):
                kv_ref[dest, a * LANE : (a + 1) * LANE] = other_ref[rows, b * LANE : (b + 1) * LANE]

    chunk = chunk_ref[j]
    low = pl.multiple_of(jnp.maximum(chunk - 4, 0) * LANE, LANE)
    width = 5 * LANE
    key_pos = low + lax.broadcasted_iota(jnp.int32, (LANE, width), 1)
    query_pos = chunk * LANE + lax.broadcasted_iota(jnp.int32, (LANE, width), 0)
    keep = (key_pos <= query_pos) & (key_pos >= start_ref[:, :1])
    keep = jnp.concatenate([keep] * 4, axis=0)
    cosine, sine = cos_ref[...], sin_ref[...]
    factor = HEAD_DIM ** (-0.5) * math.log2(math.e)
    for g in range(2):
        keys = kv_ref[pl.ds(low, width), g * LANE : (g + 1) * LANE]
        values = kv_ref[pl.ds(low, width), (2 + g) * LANE : (3 + g) * LANE]
        query = jnp.concatenate(
            [
                turned(q_ref[:, (g * 4 + h) * LANE : (g * 4 + h + 1) * LANE], cosine, sine).astype(BF16)
                for h in range(4)
            ],
            axis=0,
        )
        scores = lax.dot_general(query, keys, (((1,), (1,)), ((), ())), preferred_element_type=F32)
        scores = jnp.where(keep, scores * factor, -jnp.inf)
        weights = jnp.exp2(scores - jnp.max(scores, axis=-1, keepdims=True)).astype(BF16)
        values = jnp.concatenate([values, jnp.ones_like(values)], axis=1)
        mixed = jnp.dot(weights, values, preferred_element_type=F32)
        mixed = (mixed[:, :LANE] / mixed[:, LANE:]).astype(BF16)
        for h in range(4):
            out_ref[:, (g * 4 + h) * LANE : (g * 4 + h + 1) * LANE] = mixed[h * LANE : (h + 1) * LANE]


def attend(chunks, queries, own, other, cosine, sine, start):
    rows = lambda j, *_: (j, 0)
    whole = lambda j, *_: (0, 0)
    return pl.pallas_call(
        attend_kernel,
        grid_spec=pltpu.PrefetchScalarGridSpec(
            num_scalar_prefetch=1,
            grid=(4,),
            in_specs=[
                pl.BlockSpec((LANE, 1024), rows),
                pl.BlockSpec((512, 512), whole),
                pl.BlockSpec((512, 512), whole),
                pl.BlockSpec((LANE, LANE), rows),
                pl.BlockSpec((LANE, LANE), rows),
                pl.BlockSpec((LANE, LANE), rows),
            ],
            out_specs=pl.BlockSpec((LANE, 1024), rows),
            scratch_shapes=[pltpu.VMEM((1024, 512), BF16)],
        ),
        out_shape=jax.ShapeDtypeStruct((512, 1024), BF16),
        name="attend",
    )(chunks, queries, own, other, cosine, sine, start)


def place_kernel(where_ref, a_ref, b_ref, c_ref, d_ref, out_ref):
    for i, ref in enumerate((a_ref, b_ref, c_ref, d_ref)):
        for half in range(2):
            dst = pl.ds(pl.multiple_of(where_ref[2 * i + half] * 512, 512), 512)
            out_ref[:, dst] = ref[:, half * 512 : (half + 1) * 512]


def place(where, parts):
    full = pl.BlockSpec(memory_space=pltpu.VMEM)
    return pl.pallas_call(
        place_kernel,
        in_specs=[pl.BlockSpec(memory_space=pltpu.SMEM)] + [full] * 4,
        out_specs=full,
        out_shape=jax.ShapeDtypeStruct((LANE, 4096), BF16),
        name="place_heads",
    )(where, *parts)


def gather_x(own):
    half = own.shape[0] // 2
    before = move(own, to_x(1))
    after = move(own, to_x(-1))
    far = (move(before[:half], to_x(1)), move(after[half:], to_x(-1)))
    return jnp.concatenate([own, before, after, *far], axis=0)


def ring_z(own):
    up, down = [own], [own]
    for _ in range(3):
        up.append(move(up[-1], to_z(1)))
        down.append(move(down[-1], to_z(-1)))
    half = own.shape[0] // 2
    far = (move(up[3][:half], to_z(1)), move(down[3][half:], to_z(-1)))
    return [own, up[1], down[1], up[2], down[2], up[3], down[3], *far]


def shards(tokens, norm_gain, query_weight, key_weight, value_weight, segment_ids, out_cotangent):
    blk, seq = lax.axis_index("blk"), lax.axis_index("seq")
    z, lo, core = blk // 4, (blk // 2) % 2, blk % 2
    x, hi = seq // 2, seq % 2
    steps = jnp.array(STEPS_Z, jnp.int32)
    flip = jnp.arange(2, dtype=jnp.int32)
    zs, los, cores = (z + steps + NZ) % NZ, lo ^ flip, core ^ flip
    count_z, count_c = jnp.arange(NZ, dtype=jnp.int32), flip
    by_z = count_z[:, None, None] * 4 + count_c[None, :, None] + los[None, None, :] * 2
    by_core = cores[:, None, None] + los[None, :, None] * 2 + zs[None, None, :] * 4
    order = jnp.stack([by_z.reshape(-1), by_core.reshape(-1)]).astype(jnp.int32)
    xs = (x + jnp.array(STEPS_X, jnp.int32) + NX) % NX
    chunks = jnp.concatenate([2 * xs + hi, 2 * xs + 1 - hi]).astype(jnp.int32)

    near = [query_weight, *(move(query_weight, to_y(k)) for k in (2, 1, 3))]
    wide = all_z_and_cores(pack_queries(near))

    narrow = jnp.concatenate([key_weight, value_weight], axis=1)
    column = stack_z(zs, ring_z(narrow))
    column = [column, *(move(column, to_y(k)) for k in (2, 1, 3))]
    column += [move(piece, to_core) for piece in column]

    normed, cot = prepare(order, tokens[0], norm_gain, out_cotangent[0])
    normed = gather_x(normed)
    cot = gather_x(cot)

    place_in = (chunks[:4, None] * LANE + jnp.arange(LANE, dtype=jnp.int32)[None, :]).reshape(-1)
    half = HEAD_DIM // 2
    expo = jnp.arange(half, dtype=F32) * (2.0 / HEAD_DIM)
    freq = jnp.power(jnp.float32(500000.0), -expo)
    angle = place_in.astype(F32)[:, None] * freq[None, :]
    cosine, sine = jnp.cos(angle), jnp.sin(angle)
    cosine = jnp.concatenate([cosine, cosine], axis=1)
    sine = jnp.concatenate([-sine, sine], axis=1)
    segment = segment_ids[0]
    mine = jnp.concatenate([lax.dynamic_slice_in_dim(segment, chunks[i] * LANE, LANE) for i in range(4)])
    start = jnp.sum((segment[None, :] < mine[:, None]).astype(jnp.int32), axis=1)
    start = jnp.broadcast_to(start[:, None], (512, LANE))

    own_kv = keys_values(core, normed, column, cosine, sine)
    other_kv = move(own_kv, to_y(2))
    queries = jnp.dot(normed, wide, preferred_element_type=F32)
    heads = attend(chunks, queries, own_kv, other_kv, cosine, sine, start)

    parts = [heads[:LANE]]
    for i, step in ((2, -1), (1, 1), (3, 2)):
        parts.append(move(heads[i * LANE : (i + 1) * LANE], to_x(-step)))
    where = jnp.stack([2 * xs + hi, 2 * xs + 1 - hi], axis=1).reshape(-1).astype(jnp.int32)
    mixed = place(where, parts)

    def product(which, a, b):
        columns = cot[:, (2 * which + a) * 1024 : (2 * which + a + 1) * 1024]
        part = heads[:, b * 512 : (b + 1) * 512]
        return lax.dot_general(columns, part, (((0,), (0,)), ((), ())), preferred_element_type=F32)

    blocks = ((2, 0, 1), (1, 1, 0), (3, 1, 1), (0, 0, 0))
    from_core = [move(product(1, a, b).astype(BF16), to_core) for _, a, b in blocks]
    terms = []
    for (flip_by, a, b), other in zip(blocks, from_core):
        term = product(0, a, b) + other.astype(F32)
        terms.append(move(term.astype(BF16), to_y(flip_by)).astype(F32) if flip_by else term)
    sums = terms[3] + terms[0] + terms[1] + terms[2]
    sums = sums.astype(BF16).reshape(8, LANE, 512)
    grad = sums[0].astype(F32)
    for i in range(1, 8):
        grad = grad + move(sums[i], to_z(STEPS_Z[i])).astype(F32)
    return (mixed[None], grad)


def solution(mesh):
    return jax.shard_map(
        shards,
        mesh=mesh,
        in_specs=(
            P("blk", "seq", None),
            P(),
            P("blk", "seq"),
            P("blk", "seq"),
            P("blk", "seq"),
            P("blk", None),
            P("blk", "seq", None),
        ),
        out_specs=(P("blk", "seq", None), P("blk", "seq")),
        check_vma=False,
    )
```

```python
import math

import jax
import jax.numpy as jnp
from jax import lax
from jax.experimental import pallas as pl
from jax.experimental.pallas import tpu as pltpu
from jax.sharding import PartitionSpec as P

HEAD_DIM = 128
LANE = 128
NX, NY, NZ = 4, 4, 8
STEPS_X = (0, -1, 1, 2)
F32 = jnp.float32
BF16 = jnp.bfloat16


def move(value, target):
    pairs = []
    for blk in range(32):
        for seq in range(8):
            z, lo, core = blk // 4, (blk // 2) % 2, blk % 2
            x, hi = seq // 2, seq % 2
            tx, ty, tz, tc = target(x, hi * 2 + lo, z, core)
            tx, ty, tz = tx % NX, ty % NY, tz % NZ
            pairs.append((blk * 8 + seq, (tz * 4 + (ty % 2) * 2 + tc) * 8 + tx * 2 + ty // 2))
    return lax.ppermute(value, ("blk", "seq"), pairs)


def to_x(step):
    return lambda x, y, z, c: (x + step, y, z, c)


def to_y(flip):
    return lambda x, y, z, c: (x, y ^ flip, z, c)


def to_z(step):
    return lambda x, y, z, c: (x, y, z + step, c)


def to_core(x, y, z, c):
    return (x, y, z, 1 - c)


VMEM = pl.BlockSpec(memory_space=pltpu.VMEM)
SMEM = pl.BlockSpec(memory_space=pltpu.SMEM)
LATER = pl.BlockSpec(memory_space=pl.ANY)
BIG = pltpu.CompilerParams(vmem_limit_bytes=48 * 2**20)


def local(kernel, name, shapes, operands, specs, scratch=()):
    return pl.pallas_call(
        kernel,
        in_specs=specs,
        out_specs=jax.tree.map(lambda _: VMEM, shapes),
        out_shape=shapes,
        scratch_shapes=scratch,
        compiler_params=BIG,
        name=name,
    )(*operands)


def array(*shape):
    return jax.ShapeDtypeStruct(shape, BF16)


def lanes(block, count=1):
    return pl.ds(pl.multiple_of(block * LANE, LANE), count * LANE)


def join_columns(a, b):
    def kernel(a_ref, b_ref, out_ref):
        out_ref[:, :LANE] = a_ref[...]
        out_ref[:, LANE:] = b_ref[...]

    return local(kernel, "join_columns", array(LANE, 256), (a, b), [VMEM, VMEM])


def normalize(here, tokens, gain):
    def kernel(here_ref, tok_ref, gain_ref, out_ref):
        values = tok_ref[...].astype(F32)
        inverse = lax.rsqrt(jnp.mean(values * values, axis=-1, keepdims=True) + 1e-05)
        for j in range(32):
            z, c, l = j // 4, (j // 2) % 2, j % 2
            src = lanes(z * 4 + (here_ref[1] ^ l) * 2 + c)
            part = tok_ref[:, src].astype(F32) * inverse * gain_ref[:, src].astype(F32)
            out_ref[:, j * LANE : (j + 1) * LANE] = part.astype(BF16)

    operands = (here, tokens, gain.reshape(1, -1))
    return local(kernel, "normalize", array(*tokens.shape), operands, [SMEM, VMEM, VMEM])


def order_cotangent(here, cot, after):
    def kernel(here_ref, cot_ref, *refs):
        for j in range(32):
            c, i, l = j // 16, (j // 2) % 8, j % 2
            src = lanes(i * 4 + (here_ref[1] ^ l) * 2 + (here_ref[2] ^ c))
            refs[-1][:, j * LANE : (j + 1) * LANE] = cot_ref[:, src]

    specs = [SMEM, VMEM] + [LATER] * len(after)
    return local(kernel, "order_cotangent", array(*cot.shape), (here, cot, *after), specs)


def pack_queries(parts, after):
    def kernel(*refs):
        for i in range(4):
            rows = slice((i // 2) * LANE, (i // 2 + 1) * LANE)
            refs[-1][rows, (i % 2) * 512 : (i % 2 + 1) * 512] = refs[i][...]

    specs = [VMEM] * 4 + [LATER] * len(after)
    return local(kernel, "pack_queries", array(256, 1024), (*parts, *after), specs)


Z_GROUPS = [[z * 4 + rest for z in range(8)] for rest in range(4)]


def swap_z(blocks):
    return lax.all_to_all(blocks, "blk", 0, 0, tiled=True, axis_index_groups=Z_GROUPS)


def all_z_and_cores(block):
    groups = [[z * 4 + lo * 2 + core for z in range(8) for core in range(2)] for lo in range(2)]
    return lax.all_gather(block, "blk", axis=0, tiled=True, axis_index_groups=groups)


def ring_z(own):
    up, down = [own], [own]
    for _ in range(3):
        up.append(move(up[-1], to_z(1)))
        down.append(move(down[-1], to_z(-1)))
    half = own.shape[0] // 2
    far = (move(up[3][:half], to_z(1)), move(down[3][half:], to_z(-1)))
    return [own, up[1], down[1], up[2], down[2], up[3], down[3], *far]


def stack_z(here, parts):
    def kernel(here_ref, *refs):
        for i, step in enumerate((0, -1, 1, -2, 2, -3, 3)):
            refs[-1][lanes((here_ref[0] + step + NZ) % NZ), :] = refs[i][...]
        for half in range(2):
            row = ((here_ref[0] + 4) % NZ) * LANE + half * 64
            refs[-1][pl.ds(pl.multiple_of(row, 64), 64), :] = refs[7 + half][...]

    return local(kernel, "stack_z", array(1024, 256), (here, *parts), [SMEM] + [VMEM] * 9)


def halves(before, after, later):
    def kernel(before_ref, after_ref, _, first_ref, second_ref):
        first_ref[...] = before_ref[:64, :]
        second_ref[...] = after_ref[64:, :]

    shape = array(64, before.shape[1])
    return local(kernel, "halves", [shape, shape], (before, after, later), [VMEM, VMEM, LATER])


def gather_x(own, later):
    before = move(own, to_x(1))
    after = move(own, to_x(-1))
    first, second = halves(before, after, later)
    return own, before, after, move(first, to_x(1)), move(second, to_x(-1))


def put_rows(refs, out_ref):
    for i, ref in enumerate(refs[:3]):
        out_ref[i * LANE : (i + 1) * LANE, :] = ref[...]
    out_ref[384:448, :] = refs[3][...]
    out_ref[448:, :] = refs[4][...]


def stack_rows(parts, later):
    def kernel(*refs):
        put_rows(refs[:5], refs[-1])

    return local(kernel, "stack_rows", array(512, 4096), (*parts, later), [VMEM] * 5 + [LATER])


def turned(values, cosine, sine):
    return values * cosine + pltpu.roll(values, HEAD_DIM // 2, 1) * sine


def fill(weight_ref, piece_refs):
    for i, ref in enumerate(piece_refs):
        lo, hi = i // 2, i % 2
        for z in range(NZ):
            src = slice(z * LANE, (z + 1) * LANE)
            dst = slice(z * 256 + lo * LANE, z * 256 + (lo + 1) * LANE)
            weight_ref[dst, hi * LANE : (hi + 1) * LANE] = ref[src, :LANE]
            weight_ref[dst, (2 + hi) * LANE : (3 + hi) * LANE] = ref[src, LANE:]


def pick(x_ref, picked_ref, core):
    for z in range(NZ):
        picked_ref[:, z * 256 : (z + 1) * 256] = x_ref[:, lanes(z * 4 + core * 2, 2)]


def own_part(here, rows, pieces):
    def kernel(here_ref, *refs):
        x_out, out_ref, weight_ref, picked_ref = refs[9:]
        put_rows(refs[:5], x_out)
        fill(weight_ref, refs[5:9])
        pick(x_out, picked_ref, here_ref[2])
        out_ref[...] = jnp.dot(picked_ref[...], weight_ref[...], preferred_element_type=F32)

    scratch = [pltpu.VMEM((2048, 512), BF16), pltpu.VMEM((512, 2048), BF16)]
    shapes = [array(512, 4096), jax.ShapeDtypeStruct((512, 512), F32)]
    return local(kernel, "own_part", shapes, (here, *rows, *pieces), [SMEM] + [VMEM] * 9, scratch)


def keys_values(here, inputs, part, pieces, cosine, sine, later):
    def kernel(here_ref, x_ref, part_ref, *refs):
        cos_ref, sin_ref = refs[4:6]
        out_ref, weight_ref, picked_ref = refs[-3:]
        fill(weight_ref, refs[:4])
        pick(x_ref, picked_ref, 1 - here_ref[2])
        total = part_ref[...] + jnp.dot(picked_ref[...], weight_ref[...], preferred_element_type=F32)
        for h in range(2):
            cols = slice(h * LANE, (h + 1) * LANE)
            out_ref[:, cols] = turned(total[:, cols], cos_ref[...], sin_ref[...]).astype(BF16)
        out_ref[:, 2 * LANE :] = total[:, 2 * LANE :].astype(BF16)

    operands = (here, inputs, part, *pieces, cosine, sine, later)
    specs = [SMEM] + [VMEM] * 8 + [LATER]
    scratch = [pltpu.VMEM((2048, 512), BF16), pltpu.VMEM((512, 2048), BF16)]
    return local(kernel, "keys_values", array(512, 512), operands, specs, scratch)


def project(inputs, wide, cosine, sine):
    def kernel(x_ref, w_ref, cos_ref, sin_ref, out_ref):
        total = jnp.dot(x_ref[...], w_ref[...], preferred_element_type=F32)
        for h in range(2):
            cols = slice(h * LANE, (h + 1) * LANE)
            out_ref[:, cols] = turned(total[:, cols], cos_ref[...], sin_ref[...]).astype(BF16)

    whole = lambda t: (0, 0)
    tile = lambda t: (0, t)
    return pl.pallas_call(
        kernel,
        grid=(4,),
        in_specs=[
            pl.BlockSpec((512, 4096), whole),
            pl.BlockSpec((4096, 256), tile),
            pl.BlockSpec((512, LANE), whole),
            pl.BlockSpec((512, LANE), whole),
        ],
        out_specs=pl.BlockSpec((512, 256), tile),
        out_shape=array(512, 1024),
        compiler_params=BIG,
        name="project",
    )(inputs, wide, cosine, sine)


def attend_kernel(here_ref, q_ref, own_ref, other_ref, start_ref, out_ref, kv_ref):
    j = pl.program_id(0)
    x, hi = here_ref[3], here_ref[4]

    @pl.when(j == 0)
    def _():
        for i, step in enumerate(STEPS_X):
            rows, pair = slice(i * LANE, (i + 1) * LANE), 2 * ((x + step + NX) % NX)
            kv_ref[lanes(pair + hi), :] = own_ref[rows, :]
            for a, b in ((0, 1), (1, 0), (2, 3), (3, 2)):
                kv_ref[lanes(pair + 1 - hi), a * LANE : (a + 1) * LANE] = other_ref[rows, b * LANE : (b + 1) * LANE]

    step = jnp.where(j == 3, 2, jnp.where(j == 2, 1, -j))
    chunk = 2 * ((x + step + NX) % NX) + hi
    first = jnp.maximum(chunk - 4, 0)
    width = 5 * LANE
    key_pos = first * LANE + lax.broadcasted_iota(jnp.int32, (LANE, width), 1)
    query_pos = chunk * LANE + lax.broadcasted_iota(jnp.int32, (LANE, width), 0)
    keep = (key_pos <= query_pos) & (key_pos >= start_ref[:, :1])
    keep = jnp.concatenate([keep] * 4, axis=0)
    factor = HEAD_DIM ** (-0.5) * math.log2(math.e)
    for g in range(2):
        keys = kv_ref[lanes(first, 5), g * LANE : (g + 1) * LANE]
        values = kv_ref[lanes(first, 5), (2 + g) * LANE : (3 + g) * LANE]
        query = jnp.concatenate(
            [q_ref[:, (g * 4 + h) * LANE : (g * 4 + h + 1) * LANE] for h in range(4)], axis=0
        )
        scores = lax.dot_general(query, keys, (((1,), (1,)), ((), ())), preferred_element_type=F32)
        scores = jnp.where(keep, scores * factor, -jnp.inf)
        weights = jnp.exp2(scores - jnp.max(scores, axis=-1, keepdims=True)).astype(BF16)
        values = jnp.concatenate([values, jnp.ones_like(values)], axis=1)
        mixed = jnp.dot(weights, values, preferred_element_type=F32)
        mixed = (mixed[:, :LANE] / mixed[:, LANE:]).astype(BF16)
        for h in range(4):
            cols = slice((g * 2 + h % 2) * LANE, (g * 2 + h % 2 + 1) * LANE)
            out_ref[h // 2, :, cols] = mixed[h * LANE : (h + 1) * LANE]


def attend(here, queries, own, other, start):
    rows = lambda j, *_: (j, 0)
    whole = lambda j, *_: (0, 0)
    return pl.pallas_call(
        attend_kernel,
        grid_spec=pltpu.PrefetchScalarGridSpec(
            num_scalar_prefetch=1,
            grid=(4,),
            in_specs=[
                pl.BlockSpec((LANE, 1024), rows),
                pl.BlockSpec((512, 512), whole),
                pl.BlockSpec((512, 512), whole),
                pl.BlockSpec((LANE, LANE), rows),
            ],
            out_specs=pl.BlockSpec((2, LANE, 512), lambda j, *_: (0, j, 0)),
            scratch_shapes=[pltpu.VMEM((1024, 512), BF16)],
        ),
        out_shape=array(2, 512, 512),
        compiler_params=BIG,
        name="attend",
    )(here, queries, own, other, start)


def cut_heads(heads, later):
    def kernel(heads_ref, _, *out_refs):
        for i, ref in enumerate(out_refs):
            ref[...] = heads_ref[:, i * LANE : (i + 1) * LANE, :]

    return local(kernel, "cut_heads", [array(2, LANE, 512)] * 4, (heads, later), [VMEM, LATER])


def place_heads(here, parts):
    def kernel(here_ref, *refs):
        x, hi = here_ref[3], here_ref[4]
        for i, ref in enumerate(refs[:4]):
            pair = 2 * ((x + STEPS_X[i] + NX) % NX)
            for g in range(2):
                seq = pair + (hi if g == 0 else 1 - hi)
                for h in range(2):
                    dst = pl.ds(pl.multiple_of(seq * 512 + h * 256, 256), 256)
                    refs[4][:, dst] = ref[h, :, g * 256 : (g + 1) * 256]

    return local(kernel, "place_heads", array(LANE, 4096), (here, *parts), [SMEM] + [VMEM] * 4)


def add(a, b):
    return a.astype(F32) + b.astype(F32)


def sum_y(block):
    sent = [move(block[a, b], to_y(flip)) for flip, a, b in ((2, 0, 1), (1, 1, 0), (3, 1, 1))]
    return [*sent, block[0, 0]]


def add_parts(parts, later):
    def kernel(*refs):
        refs[-1][...] = total_of([ref[...] for ref in refs[:4]]).astype(BF16)

    operands = (*parts, *later)
    specs = [VMEM] * 4 + [LATER] * len(later)
    return local(kernel, "add_parts", array(NZ, LANE, 256), operands, specs)


def total_of(parts):
    total = parts[0].astype(F32)
    for part in parts[1:]:
        total = total + part.astype(F32)
    return total


def shards(tokens, norm_gain, query_weight, key_weight, value_weight, segment_ids, out_cotangent):
    blk, seq = lax.axis_index("blk"), lax.axis_index("seq")
    x, hi = seq // 2, seq % 2
    here = jnp.stack([blk // 4, (blk // 2) % 2, blk % 2, x, hi]).astype(jnp.int32)

    ring = ring_z(join_columns(key_weight, value_weight))
    column = stack_z(here, ring)
    near = [query_weight, *(move(query_weight, to_y(k)) for k in (2, 1, 3))]
    normed = normalize(here, tokens[0], norm_gain)
    wide = all_z_and_cores(pack_queries(near, (normed, ring[1], ring[2])))

    rows = gather_x(normed, column)
    pieces = [column, *(move(column, to_y(k)) for k in (2, 1, 3))]
    other_pieces = [move(piece, to_core) for piece in pieces]

    chunks = 2 * ((x + jnp.array(STEPS_X, jnp.int32) + NX) % NX) + hi
    place_in = (chunks[:, None] * LANE + jnp.arange(LANE, dtype=jnp.int32)[None, :]).reshape(-1)
    half = HEAD_DIM // 2
    expo = jnp.arange(half, dtype=F32) * (2.0 / HEAD_DIM)
    freq = jnp.power(jnp.float32(500000.0), -expo)
    angle = place_in.astype(F32)[:, None] * freq[None, :]
    cosine, sine = jnp.cos(angle), jnp.sin(angle)
    cosine = jnp.concatenate([cosine, cosine], axis=1)
    sine = jnp.concatenate([-sine, sine], axis=1)
    segment = segment_ids[0]
    mine = jnp.concatenate([lax.dynamic_slice_in_dim(segment, chunks[i] * LANE, LANE) for i in range(4)])
    start = jnp.sum((segment[None, :] < mine[:, None]).astype(jnp.int32), axis=1)
    start = jnp.broadcast_to(start[:, None], (512, LANE))

    inputs, part = own_part(here, rows, pieces)
    own_kv = keys_values(here, inputs, part, other_pieces, cosine, sine, start)
    other_kv = move(own_kv, to_y(2))
    queries = project(inputs, wide, cosine, sine)
    cot = gather_x(order_cotangent(here, out_cotangent[0], rows[1:3]), own_kv)
    heads = attend(here, queries, own_kv, other_kv, start)
    cot = stack_rows(cot, heads)

    def product(core, half):
        columns = cot[:, core * 2048 : (core + 1) * 2048]
        return lax.dot_general(columns, heads[half], (((0,), (0,)), ((), ())), preferred_element_type=F32)

    from_core = [move(product(1, half).astype(BF16), to_core) for half in range(2)]
    first, second = (add(product(0, half), from_core[half]).astype(BF16) for half in range(2))
    quarters = [(a, b) for a in range(2) for b in range(2)]
    second = lax.psum_scatter(
        second, "blk", scatter_dimension=0, tiled=True, axis_index_groups=Z_GROUPS
    )
    first = first.reshape(8, 2, LANE, 512)
    first = sum_y({(a, b): first[:, a, :, b * 256 : (b + 1) * 256] for a, b in quarters})
    chunks = cut_heads(heads, first[1])
    parts = [chunks[0], *(move(chunks[i], to_x(-step)) for i, step in ((2, -1), (1, 1), (3, 2)))]
    mixed = place_heads(here, parts)
    first = swap_z(add_parts(first, parts[1:]))
    left = jnp.sum(first.astype(F32), axis=0)
    second = sum_y({(a, b): second[a * LANE : (a + 1) * LANE, b * 256 : (b + 1) * 256] for a, b in quarters})
    return (mixed[None], jnp.concatenate([left, total_of(second)], axis=1))


def solution(mesh):
    return jax.shard_map(
        shards,
        mesh=mesh,
        in_specs=(
            P("blk", "seq", None),
            P(),
            P("blk", "seq"),
            P("blk", "seq"),
            P("blk", "seq"),
            P("blk", None),
            P("blk", "seq", None),
        ),
        out_specs=(P("blk", "seq", None), P("blk", "seq")),
        check_vma=False,
    )
```

```python
import math

import jax
import jax.numpy as jnp
from jax import lax
from jax.experimental import pallas as pl
from jax.experimental.pallas import tpu as pltpu
from jax.sharding import PartitionSpec as P

HEAD_DIM = 128
LANE = 128
NX, NY, NZ = 4, 4, 8
STEPS_X = (0, -1, 1, 2)
F32 = jnp.float32
BF16 = jnp.bfloat16


def move(value, target):
    pairs = []
    for blk in range(32):
        for seq in range(8):
            z, lo, core = blk // 4, (blk // 2) % 2, blk % 2
            x, hi = seq // 2, seq % 2
            tx, ty, tz, tc = target(x, hi * 2 + lo, z, core)
            tx, ty, tz = tx % NX, ty % NY, tz % NZ
            pairs.append((blk * 8 + seq, (tz * 4 + (ty % 2) * 2 + tc) * 8 + tx * 2 + ty // 2))
    return lax.ppermute(value, ("blk", "seq"), pairs)


def to_x(step):
    return lambda x, y, z, c: (x + step, y, z, c)


def to_y(flip):
    return lambda x, y, z, c: (x, y ^ flip, z, c)


def to_z(step):
    return lambda x, y, z, c: (x, y, z + step, c)


def to_core(x, y, z, c):
    return (x, y, z, 1 - c)


VMEM = pl.BlockSpec(memory_space=pltpu.VMEM)
SMEM = pl.BlockSpec(memory_space=pltpu.SMEM)
LATER = pl.BlockSpec(memory_space=pl.ANY)
BIG = pltpu.CompilerParams(vmem_limit_bytes=48 * 2**20)


def local(kernel, name, shapes, operands, specs, scratch=()):
    return pl.pallas_call(
        kernel,
        in_specs=specs,
        out_specs=jax.tree.map(lambda _: VMEM, shapes),
        out_shape=shapes,
        scratch_shapes=scratch,
        compiler_params=BIG,
        name=name,
    )(*operands)


def array(*shape):
    return jax.ShapeDtypeStruct(shape, BF16)


def lanes(block, count=1):
    return pl.ds(pl.multiple_of(block * LANE, LANE), count * LANE)


def join_columns(a, b):
    def kernel(a_ref, b_ref, out_ref):
        out_ref[:, :LANE] = a_ref[...]
        out_ref[:, LANE:] = b_ref[...]

    return local(kernel, "join_columns", array(LANE, 256), (a, b), [VMEM, VMEM])


def normalize(here, tokens, gain):
    def kernel(here_ref, tok_ref, gain_ref, out_ref):
        values = tok_ref[...].astype(F32)
        inverse = lax.rsqrt(jnp.mean(values * values, axis=-1, keepdims=True) + 1e-05)
        for j in range(32):
            z, c, l = j // 4, (j // 2) % 2, j % 2
            src = lanes(z * 4 + (here_ref[1] ^ l) * 2 + c)
            part = tok_ref[:, src].astype(F32) * inverse * gain_ref[:, src].astype(F32)
            out_ref[:, j * LANE : (j + 1) * LANE] = part.astype(BF16)

    operands = (here, tokens, gain.reshape(1, -1))
    return local(kernel, "normalize", array(*tokens.shape), operands, [SMEM, VMEM, VMEM])


def order_cotangent(here, cot, after):
    def kernel(here_ref, cot_ref, *refs):
        for j in range(32):
            c, i, l = j // 16, (j // 2) % 8, j % 2
            src = lanes(i * 4 + (here_ref[1] ^ l) * 2 + (here_ref[2] ^ c))
            refs[c - 2][:, j % 16 * LANE : (j % 16 + 1) * LANE] = cot_ref[:, src]

    specs = [SMEM, VMEM] + [LATER] * len(after)
    return local(kernel, "order_cotangent", [array(LANE, 2048)] * 2, (here, cot, *after), specs)


def pack_queries(parts, after):
    def kernel(*refs):
        for i in range(4):
            rows = slice((i // 2) * LANE, (i // 2 + 1) * LANE)
            refs[-1][rows, (i % 2) * 512 : (i % 2 + 1) * 512] = refs[i][...]

    specs = [VMEM] * 4 + [LATER] * len(after)
    return local(kernel, "pack_queries", array(256, 1024), (*parts, *after), specs)


Z_GROUPS = [[z * 4 + rest for z in range(8)] for rest in range(4)]


def swap_z(blocks):
    return lax.all_to_all(blocks, "blk", 0, 0, tiled=True, axis_index_groups=Z_GROUPS)


def all_z_and_cores(block):
    groups = [[z * 4 + lo * 2 + core for z in range(8) for core in range(2)] for lo in range(2)]
    return lax.all_gather(block, "blk", axis=0, tiled=True, axis_index_groups=groups)


def ring_z(own):
    up, down = [own], [own]
    for _ in range(3):
        up.append(move(up[-1], to_z(1)))
        down.append(move(down[-1], to_z(-1)))
    half = own.shape[0] // 2
    far = (move(up[3][:half], to_z(1)), move(down[3][half:], to_z(-1)))
    return [own, up[1], down[1], up[2], down[2], up[3], down[3], *far]


def stack_z(here, parts):
    def kernel(here_ref, *refs):
        for i, step in enumerate((0, -1, 1, -2, 2, -3, 3)):
            refs[-1][lanes((here_ref[0] + step + NZ) % NZ), :] = refs[i][...]
        for half in range(2):
            row = ((here_ref[0] + 4) % NZ) * LANE + half * 64
            refs[-1][pl.ds(pl.multiple_of(row, 64), 64), :] = refs[7 + half][...]

    return local(kernel, "stack_z", array(1024, 256), (here, *parts), [SMEM] + [VMEM] * 9)


def halves(before, after, later):
    def kernel(before_ref, after_ref, _, first_ref, second_ref):
        first_ref[...] = before_ref[:64, :]
        second_ref[...] = after_ref[64:, :]

    shape = array(64, before.shape[1])
    return local(kernel, "halves", [shape, shape], (before, after, later), [VMEM, VMEM, LATER])


def gather_x(own, later):
    before = move(own, to_x(1))
    after = move(own, to_x(-1))
    first, second = halves(before, after, later)
    return (own, before, after, move(first, to_x(1)), move(second, to_x(-1))), (first, second)


def put_rows(refs, out_ref):
    for i, ref in enumerate(refs[:3]):
        out_ref[i * LANE : (i + 1) * LANE, :] = ref[...]
    out_ref[384:448, :] = refs[3][...]
    out_ref[448:, :] = refs[4][...]


def stack_rows(parts, later):
    def kernel(*refs):
        put_rows(refs[:5], refs[-1])

    shape = array(512, parts[0].shape[1])
    return local(kernel, "stack_rows", shape, (*parts, later), [VMEM] * 5 + [LATER])


def turned(values, cosine, sine):
    return values * cosine + pltpu.roll(values, HEAD_DIM // 2, 1) * sine


def fill(weight_ref, piece_refs):
    for i, ref in enumerate(piece_refs):
        lo, hi = i // 2, i % 2
        for z in range(NZ):
            src = slice(z * LANE, (z + 1) * LANE)
            dst = slice(z * 256 + lo * LANE, z * 256 + (lo + 1) * LANE)
            weight_ref[dst, hi * LANE : (hi + 1) * LANE] = ref[src, :LANE]
            weight_ref[dst, (2 + hi) * LANE : (3 + hi) * LANE] = ref[src, LANE:]


def pick(x_ref, picked_ref, core):
    for z in range(NZ):
        picked_ref[:, z * 256 : (z + 1) * 256] = x_ref[:, lanes(z * 4 + core * 2, 2)]


def own_part(here, rows, pieces):
    def kernel(here_ref, *refs):
        x_out, out_ref, weight_ref, picked_ref = refs[9:]
        put_rows(refs[:5], x_out)
        fill(weight_ref, refs[5:9])
        pick(x_out, picked_ref, here_ref[2])
        out_ref[...] = jnp.dot(picked_ref[...], weight_ref[...], preferred_element_type=F32)

    scratch = [pltpu.VMEM((2048, 512), BF16), pltpu.VMEM((512, 2048), BF16)]
    shapes = [array(512, 4096), jax.ShapeDtypeStruct((512, 512), F32)]
    return local(kernel, "own_part", shapes, (here, *rows, *pieces), [SMEM] + [VMEM] * 9, scratch)


def keys_values(here, inputs, part, pieces, cosine, sine, later):
    def kernel(here_ref, x_ref, part_ref, *refs):
        cos_ref, sin_ref = refs[4:6]
        out_ref, weight_ref, picked_ref = refs[-3:]
        fill(weight_ref, refs[:4])
        pick(x_ref, picked_ref, 1 - here_ref[2])
        total = part_ref[...] + jnp.dot(picked_ref[...], weight_ref[...], preferred_element_type=F32)
        for h in range(2):
            cols = slice(h * LANE, (h + 1) * LANE)
            out_ref[:, cols] = turned(total[:, cols], cos_ref[...], sin_ref[...]).astype(BF16)
        out_ref[:, 2 * LANE :] = total[:, 2 * LANE :].astype(BF16)

    operands = (here, inputs, part, *pieces, cosine, sine, later)
    specs = [SMEM] + [VMEM] * 8 + [LATER]
    scratch = [pltpu.VMEM((2048, 512), BF16), pltpu.VMEM((512, 2048), BF16)]
    return local(kernel, "keys_values", array(512, 512), operands, specs, scratch)


def project(inputs, wide, cosine, sine):
    def kernel(x_ref, w_ref, cos_ref, sin_ref, out_ref):
        total = jnp.dot(x_ref[...], w_ref[...], preferred_element_type=F32)
        for h in range(2):
            cols = slice(h * LANE, (h + 1) * LANE)
            out_ref[:, cols] = turned(total[:, cols], cos_ref[...], sin_ref[...]).astype(BF16)

    whole = lambda t: (0, 0)
    tile = lambda t: (0, t)
    return pl.pallas_call(
        kernel,
        grid=(4,),
        in_specs=[
            pl.BlockSpec((512, 4096), whole),
            pl.BlockSpec((4096, 256), tile),
            pl.BlockSpec((512, LANE), whole),
            pl.BlockSpec((512, LANE), whole),
        ],
        out_specs=pl.BlockSpec((512, 256), tile),
        out_shape=array(512, 1024),
        compiler_params=BIG,
        name="project",
    )(inputs, wide, cosine, sine)


def attend_kernel(here_ref, q_ref, own_ref, other_ref, start_ref, _a, _b, out_ref, kv_ref):
    j = pl.program_id(0)
    x, hi = here_ref[3], here_ref[4]

    @pl.when(j == 0)
    def _():
        for i, step in enumerate(STEPS_X):
            rows, pair = slice(i * LANE, (i + 1) * LANE), 2 * ((x + step + NX) % NX)
            kv_ref[lanes(pair + hi), :] = own_ref[rows, :]
            for a, b in ((0, 1), (1, 0), (2, 3), (3, 2)):
                kv_ref[lanes(pair + 1 - hi), a * LANE : (a + 1) * LANE] = other_ref[rows, b * LANE : (b + 1) * LANE]

    step = jnp.where(j == 3, 2, jnp.where(j == 2, 1, -j))
    chunk = 2 * ((x + step + NX) % NX) + hi
    first = jnp.maximum(chunk - 4, 0)
    width = 5 * LANE
    key_pos = first * LANE + lax.broadcasted_iota(jnp.int32, (LANE, width), 1)
    query_pos = chunk * LANE + lax.broadcasted_iota(jnp.int32, (LANE, width), 0)
    keep = (key_pos <= query_pos) & (key_pos >= start_ref[:, :1])
    keep = jnp.concatenate([keep] * 4, axis=0)
    factor = HEAD_DIM ** (-0.5) * math.log2(math.e)
    for g in range(2):
        keys = kv_ref[lanes(first, 5), g * LANE : (g + 1) * LANE]
        values = kv_ref[lanes(first, 5), (2 + g) * LANE : (3 + g) * LANE]
        query = jnp.concatenate(
            [q_ref[:, (g * 4 + h) * LANE : (g * 4 + h + 1) * LANE] for h in range(4)], axis=0
        )
        scores = lax.dot_general(query, keys, (((1,), (1,)), ((), ())), preferred_element_type=F32)
        scores = jnp.where(keep, scores * factor, -jnp.inf)
        weights = jnp.exp2(scores - jnp.max(scores, axis=-1, keepdims=True)).astype(BF16)
        values = jnp.concatenate([values, jnp.ones_like(values)], axis=1)
        mixed = jnp.dot(weights, values, preferred_element_type=F32)
        mixed = (mixed[:, :LANE] / mixed[:, LANE:]).astype(BF16)
        for h in range(4):
            cols = slice((g * 2 + h % 2) * LANE, (g * 2 + h % 2 + 1) * LANE)
            out_ref[h // 2, :, cols] = mixed[h * LANE : (h + 1) * LANE]


def attend(here, queries, own, other, start, later):
    rows = lambda j, *_: (j, 0)
    whole = lambda j, *_: (0, 0)
    return pl.pallas_call(
        attend_kernel,
        grid_spec=pltpu.PrefetchScalarGridSpec(
            num_scalar_prefetch=1,
            grid=(4,),
            in_specs=[
                pl.BlockSpec((LANE, 1024), rows),
                pl.BlockSpec((512, 512), whole),
                pl.BlockSpec((512, 512), whole),
                pl.BlockSpec((LANE, LANE), rows),
                LATER,
                LATER,
            ],
            out_specs=pl.BlockSpec((2, LANE, 512), lambda j, *_: (0, j, 0)),
            scratch_shapes=[pltpu.VMEM((1024, 512), BF16)],
        ),
        out_shape=array(2, 512, 512),
        compiler_params=BIG,
        name="attend",
    )(here, queries, own, other, start, *later)


def cut_heads(heads, later):
    def kernel(heads_ref, _, *out_refs):
        for i, ref in enumerate(out_refs):
            ref[...] = heads_ref[:, i * LANE : (i + 1) * LANE, :]

    return local(kernel, "cut_heads", [array(2, LANE, 512)] * 4, (heads, later), [VMEM, LATER])


def place_heads(here, parts):
    def kernel(here_ref, *refs):
        x, hi = here_ref[3], here_ref[4]
        for i, ref in enumerate(refs[:4]):
            pair = 2 * ((x + STEPS_X[i] + NX) % NX)
            for g in range(2):
                seq = pair + (hi if g == 0 else 1 - hi)
                for h in range(2):
                    dst = pl.ds(pl.multiple_of(seq * 512 + h * 256, 256), 256)
                    refs[4][:, dst] = ref[h, :, g * 256 : (g + 1) * 256]

    return local(kernel, "place_heads", array(LANE, 4096), (here, *parts), [SMEM] + [VMEM] * 4)


def add(a, b):
    return a.astype(F32) + b.astype(F32)


def sum_y(block):
    sent = [move(block[a, b], to_y(flip)) for flip, a, b in ((2, 0, 1), (1, 1, 0), (3, 1, 1))]
    return [*sent, block[0, 0]]


def add_parts(parts, later):
    def kernel(*refs):
        refs[-1][...] = total_of([ref[...] for ref in refs[:4]]).astype(BF16)

    operands = (*parts, *later)
    specs = [VMEM] * 4 + [LATER] * len(later)
    return local(kernel, "add_parts", array(NZ, LANE, 256), operands, specs)


def total_of(parts):
    total = parts[0].astype(F32)
    for part in parts[1:]:
        total = total + part.astype(F32)
    return total


def shards(tokens, norm_gain, query_weight, key_weight, value_weight, segment_ids, out_cotangent):
    blk, seq = lax.axis_index("blk"), lax.axis_index("seq")
    x, hi = seq // 2, seq % 2
    here = jnp.stack([blk // 4, (blk // 2) % 2, blk % 2, x, hi]).astype(jnp.int32)

    ring = ring_z(join_columns(key_weight, value_weight))
    column = stack_z(here, ring)
    near = [query_weight, *(move(query_weight, to_y(k)) for k in (2, 1, 3))]
    normed = normalize(here, tokens[0], norm_gain)
    wide = all_z_and_cores(pack_queries(near, (normed, ring[1], ring[2])))

    rows, _ = gather_x(normed, column)
    pieces = [column, *(move(column, to_y(k)) for k in (2, 1, 3))]
    other_pieces = [move(piece, to_core) for piece in pieces]

    chunks = 2 * ((x + jnp.array(STEPS_X, jnp.int32) + NX) % NX) + hi
    place_in = (chunks[:, None] * LANE + jnp.arange(LANE, dtype=jnp.int32)[None, :]).reshape(-1)
    half = HEAD_DIM // 2
    expo = jnp.arange(half, dtype=F32) * (2.0 / HEAD_DIM)
    freq = jnp.power(jnp.float32(500000.0), -expo)
    angle = place_in.astype(F32)[:, None] * freq[None, :]
    cosine, sine = jnp.cos(angle), jnp.sin(angle)
    cosine = jnp.concatenate([cosine, cosine], axis=1)
    sine = jnp.concatenate([-sine, sine], axis=1)
    segment = segment_ids[0]
    mine = jnp.concatenate([lax.dynamic_slice_in_dim(segment, chunks[i] * LANE, LANE) for i in range(4)])
    start = jnp.sum((segment[None, :] < mine[:, None]).astype(jnp.int32), axis=1)
    start = jnp.broadcast_to(start[:, None], (512, LANE))

    inputs, part = own_part(here, rows, pieces)
    own_kv = keys_values(here, inputs, part, other_pieces, cosine, sine, start)
    other_kv = move(own_kv, to_y(2))
    queries = project(inputs, wide, cosine, sine)
    cot_own, cot_other = order_cotangent(here, out_cotangent[0], rows[1:3])
    cot_other, _ = gather_x(cot_other, own_kv)
    cot_own, sent = gather_x(cot_own, queries)
    cot_other = stack_rows(cot_other, queries)
    heads = attend(here, queries, own_kv, other_kv, start, sent)
    cot_own = stack_rows(cot_own, heads)

    def product(columns, half):
        return lax.dot_general(columns, heads[half], (((0,), (0,)), ((), ())), preferred_element_type=F32)

    from_core = [move(product(cot_other, half).astype(BF16), to_core) for half in range(2)]
    first, second = (add(product(cot_own, half), from_core[half]).astype(BF16) for half in range(2))
    quarters = [(a, b) for a in range(2) for b in range(2)]
    second = lax.psum_scatter(
        second, "blk", scatter_dimension=0, tiled=True, axis_index_groups=Z_GROUPS
    )
    first = first.reshape(8, 2, LANE, 512)
    first = sum_y({(a, b): first[:, a, :, b * 256 : (b + 1) * 256] for a, b in quarters})
    chunks = cut_heads(heads, first[1])
    parts = [chunks[0], *(move(chunks[i], to_x(-step)) for i, step in ((2, -1), (1, 1), (3, 2)))]
    mixed = place_heads(here, parts)
    first = swap_z(add_parts(first, parts[1:]))
    left = jnp.sum(first.astype(F32), axis=0)
    second = sum_y({(a, b): second[a * LANE : (a + 1) * LANE, b * 256 : (b + 1) * 256] for a, b in quarters})
    return (mixed[None], jnp.concatenate([left, total_of(second)], axis=1))


def solution(mesh):
    return jax.shard_map(
        shards,
        mesh=mesh,
        in_specs=(
            P("blk", "seq", None),
            P(),
            P("blk", "seq"),
            P("blk", "seq"),
            P("blk", "seq"),
            P("blk", None),
            P("blk", "seq", None),
        ),
        out_specs=(P("blk", "seq", None), P("blk", "seq")),
        check_vma=False,
    )
```

```python
import math

import jax
import jax.numpy as jnp
from jax import lax
from jax.experimental import pallas as pl
from jax.experimental.pallas import tpu as pltpu
from jax.sharding import PartitionSpec as P

HEAD_DIM = 128
LANE = 128
NX, NY, NZ = 4, 4, 8
STEPS_X = (0, -1, 1, 2)
F32 = jnp.float32
BF16 = jnp.bfloat16


def move(value, target):
    pairs = []
    for blk in range(32):
        for seq in range(8):
            z, lo, core = blk // 4, (blk // 2) % 2, blk % 2
            x, hi = seq // 2, seq % 2
            tx, ty, tz, tc = target(x, hi * 2 + lo, z, core)
            tx, ty, tz = tx % NX, ty % NY, tz % NZ
            pairs.append((blk * 8 + seq, (tz * 4 + (ty % 2) * 2 + tc) * 8 + tx * 2 + ty // 2))
    return lax.ppermute(value, ("blk", "seq"), pairs)


def to_x(step):
    return lambda x, y, z, c: (x + step, y, z, c)


def to_y(flip):
    return lambda x, y, z, c: (x, y ^ flip, z, c)


def to_z(step):
    return lambda x, y, z, c: (x, y, z + step, c)


def to_core(x, y, z, c):
    return (x, y, z, 1 - c)


VMEM = pl.BlockSpec(memory_space=pltpu.VMEM)
SMEM = pl.BlockSpec(memory_space=pltpu.SMEM)
LATER = pl.BlockSpec(memory_space=pl.ANY)
BIG = pltpu.CompilerParams(vmem_limit_bytes=48 * 2**20)


def local(kernel, name, shapes, operands, specs, scratch=()):
    return pl.pallas_call(
        kernel,
        in_specs=specs,
        out_specs=jax.tree.map(lambda _: VMEM, shapes),
        out_shape=shapes,
        scratch_shapes=scratch,
        compiler_params=BIG,
        name=name,
    )(*operands)


def array(*shape):
    return jax.ShapeDtypeStruct(shape, BF16)


def lanes(block, count=1):
    return pl.ds(pl.multiple_of(block * LANE, LANE), count * LANE)


def join_columns(a, b):
    def kernel(a_ref, b_ref, out_ref):
        out_ref[:, :LANE] = a_ref[...]
        out_ref[:, LANE:] = b_ref[...]

    return local(kernel, "join_columns", array(LANE, 256), (a, b), [VMEM, VMEM])


def normalize(here, tokens, gain):
    def kernel(here_ref, tok_ref, gain_ref, out_ref):
        values = tok_ref[...].astype(F32)
        inverse = lax.rsqrt(jnp.mean(values * values, axis=-1, keepdims=True) + 1e-05)
        for j in range(32):
            z, c, l = j // 4, (j // 2) % 2, j % 2
            src = lanes(z * 4 + (here_ref[1] ^ l) * 2 + c)
            part = tok_ref[:, src].astype(F32) * inverse * gain_ref[:, src].astype(F32)
            out_ref[:, j * LANE : (j + 1) * LANE] = part.astype(BF16)

    operands = (here, tokens, gain.reshape(1, -1))
    return local(kernel, "normalize", array(*tokens.shape), operands, [SMEM, VMEM, VMEM])


def order_cotangent(here, cot, after):
    def kernel(here_ref, cot_ref, *refs):
        for j in range(32):
            c, i, l = j // 16, (j // 2) % 8, j % 2
            src = lanes(i * 4 + (here_ref[1] ^ l) * 2 + (here_ref[2] ^ c))
            refs[c - 2][:, j % 16 * LANE : (j % 16 + 1) * LANE] = cot_ref[:, src]

    specs = [SMEM, VMEM] + [LATER] * len(after)
    return local(kernel, "order_cotangent", [array(LANE, 2048)] * 2, (here, cot, *after), specs)


def pack_queries(parts, after):
    def kernel(*refs):
        for i in range(4):
            rows = slice((i // 2) * LANE, (i // 2 + 1) * LANE)
            refs[-1][rows, (i % 2) * 512 : (i % 2 + 1) * 512] = refs[i][...]

    specs = [VMEM] * 4 + [LATER] * len(after)
    return local(kernel, "pack_queries", array(256, 1024), (*parts, *after), specs)


Z_GROUPS = [[z * 4 + rest for z in range(8)] for rest in range(4)]


def swap_z(blocks):
    return lax.all_to_all(blocks, "blk", 0, 0, tiled=True, axis_index_groups=Z_GROUPS)


def all_z_and_cores(block):
    groups = [[z * 4 + lo * 2 + core for z in range(8) for core in range(2)] for lo in range(2)]
    return lax.all_gather(block, "blk", axis=0, tiled=True, axis_index_groups=groups)


def ring_z(own):
    up, down = [own], [own]
    for _ in range(3):
        up.append(move(up[-1], to_z(1)))
        down.append(move(down[-1], to_z(-1)))
    half = own.shape[0] // 2
    far = (move(up[3][:half], to_z(1)), move(down[3][half:], to_z(-1)))
    return [own, up[1], down[1], up[2], down[2], up[3], down[3], *far]


def stack_z(here, parts):
    def kernel(here_ref, *refs):
        for i, step in enumerate((0, -1, 1, -2, 2, -3, 3)):
            refs[-1][lanes((here_ref[0] + step + NZ) % NZ), :] = refs[i][...]
        for half in range(2):
            row = ((here_ref[0] + 4) % NZ) * LANE + half * 64
            refs[-1][pl.ds(pl.multiple_of(row, 64), 64), :] = refs[7 + half][...]

    return local(kernel, "stack_z", array(1024, 256), (here, *parts), [SMEM] + [VMEM] * 9)


def halves(before, after, later):
    def kernel(before_ref, after_ref, _, first_ref, second_ref):
        first_ref[...] = before_ref[:64, :]
        second_ref[...] = after_ref[64:, :]

    shape = array(64, before.shape[1])
    return local(kernel, "halves", [shape, shape], (before, after, later), [VMEM, VMEM, LATER])


def gather_x(own, later):
    before = move(own, to_x(1))
    after = move(own, to_x(-1))
    first, second = halves(before, after, later)
    return (own, before, after, move(first, to_x(1)), move(second, to_x(-1))), (first, second)


def put_rows(refs, out_ref):
    for i, ref in enumerate(refs[:3]):
        out_ref[i * LANE : (i + 1) * LANE, :] = ref[...]
    out_ref[384:448, :] = refs[3][...]
    out_ref[448:, :] = refs[4][...]


def stack_rows(parts, later):
    def kernel(*refs):
        put_rows(refs[:5], refs[-1])

    shape = array(512, parts[0].shape[1])
    return local(kernel, "stack_rows", shape, (*parts, later), [VMEM] * 5 + [LATER])


def turned(values, cosine, sine):
    return values * cosine + pltpu.roll(values, HEAD_DIM // 2, 1) * sine


def fill(weight_ref, piece_refs):
    for i, ref in enumerate(piece_refs):
        lo, hi = i // 2, i % 2
        for z in range(NZ):
            src = slice(z * LANE, (z + 1) * LANE)
            dst = slice(z * 256 + lo * LANE, z * 256 + (lo + 1) * LANE)
            weight_ref[dst, hi * LANE : (hi + 1) * LANE] = ref[src, :LANE]
            weight_ref[dst, (2 + hi) * LANE : (3 + hi) * LANE] = ref[src, LANE:]


def pick(x_ref, picked_ref, core):
    for z in range(NZ):
        picked_ref[:, z * 256 : (z + 1) * 256] = x_ref[:, lanes(z * 4 + core * 2, 2)]


def own_part(here, rows, pieces):
    def kernel(here_ref, *refs):
        x_out, out_ref, weight_ref, picked_ref = refs[9:]
        put_rows(refs[:5], x_out)
        fill(weight_ref, refs[5:9])
        pick(x_out, picked_ref, here_ref[2])
        out_ref[...] = jnp.dot(picked_ref[...], weight_ref[...], preferred_element_type=F32)

    scratch = [pltpu.VMEM((2048, 512), BF16), pltpu.VMEM((512, 2048), BF16)]
    shapes = [array(512, 4096), jax.ShapeDtypeStruct((512, 512), F32)]
    return local(kernel, "own_part", shapes, (here, *rows, *pieces), [SMEM] + [VMEM] * 9, scratch)


def keys_values(here, inputs, part, pieces, cosine, sine, later):
    def kernel(here_ref, x_ref, part_ref, *refs):
        cos_ref, sin_ref = refs[4:6]
        out_ref, weight_ref, picked_ref = refs[-3:]
        fill(weight_ref, refs[:4])
        pick(x_ref, picked_ref, 1 - here_ref[2])
        total = part_ref[...] + jnp.dot(picked_ref[...], weight_ref[...], preferred_element_type=F32)
        for h in range(2):
            cols = slice(h * LANE, (h + 1) * LANE)
            out_ref[:, cols] = turned(total[:, cols], cos_ref[...], sin_ref[...]).astype(BF16)
        out_ref[:, 2 * LANE :] = total[:, 2 * LANE :].astype(BF16)

    operands = (here, inputs, part, *pieces, cosine, sine, later)
    specs = [SMEM] + [VMEM] * 8 + [LATER]
    scratch = [pltpu.VMEM((2048, 512), BF16), pltpu.VMEM((512, 2048), BF16)]
    return local(kernel, "keys_values", array(512, 512), operands, specs, scratch)


def project(inputs, wide, cosine, sine):
    def kernel(x_ref, w_ref, cos_ref, sin_ref, out_ref):
        total = jnp.dot(x_ref[...], w_ref[...], preferred_element_type=F32)
        for h in range(2):
            cols = slice(h * LANE, (h + 1) * LANE)
            out_ref[:, cols] = turned(total[:, cols], cos_ref[...], sin_ref[...]).astype(BF16)

    whole = lambda t: (0, 0)
    tile = lambda t: (0, t)
    return pl.pallas_call(
        kernel,
        grid=(4,),
        in_specs=[
            pl.BlockSpec((512, 4096), whole),
            pl.BlockSpec((4096, 256), tile),
            pl.BlockSpec((512, LANE), whole),
            pl.BlockSpec((512, LANE), whole),
        ],
        out_specs=pl.BlockSpec((512, 256), tile),
        out_shape=array(512, 1024),
        compiler_params=BIG,
        name="project",
    )(inputs, wide, cosine, sine)


def attend_kernel(here_ref, q_ref, own_ref, other_ref, start_ref, _a, _b, out_ref, kv_ref):
    j = pl.program_id(0)
    x, hi = here_ref[3], here_ref[4]

    @pl.when(j == 0)
    def _():
        for i, step in enumerate(STEPS_X):
            rows, pair = slice(i * LANE, (i + 1) * LANE), 2 * ((x + step + NX) % NX)
            kv_ref[lanes(pair + hi), :] = own_ref[rows, :]
            for a, b in ((0, 1), (1, 0), (2, 3), (3, 2)):
                kv_ref[lanes(pair + 1 - hi), a * LANE : (a + 1) * LANE] = other_ref[rows, b * LANE : (b + 1) * LANE]

    step = jnp.where(j == 3, 2, jnp.where(j == 2, 1, -j))
    chunk = 2 * ((x + step + NX) % NX) + hi
    first = jnp.maximum(chunk - 4, 0)
    width = 5 * LANE
    key_pos = first * LANE + lax.broadcasted_iota(jnp.int32, (LANE, width), 1)
    query_pos = chunk * LANE + lax.broadcasted_iota(jnp.int32, (LANE, width), 0)
    keep = (key_pos <= query_pos) & (key_pos >= start_ref[:, :1])
    keep = jnp.concatenate([keep] * 4, axis=0)
    factor = HEAD_DIM ** (-0.5) * math.log2(math.e)
    for g in range(2):
        keys = kv_ref[lanes(first, 5), g * LANE : (g + 1) * LANE]
        values = kv_ref[lanes(first, 5), (2 + g) * LANE : (3 + g) * LANE]
        query = jnp.concatenate(
            [q_ref[:, (g * 4 + h) * LANE : (g * 4 + h + 1) * LANE] for h in range(4)], axis=0
        )
        scores = lax.dot_general(query, keys, (((1,), (1,)), ((), ())), preferred_element_type=F32)
        scores = jnp.where(keep, scores * factor, -jnp.inf)
        weights = jnp.exp2(scores - jnp.max(scores, axis=-1, keepdims=True)).astype(BF16)
        values = jnp.concatenate([values, jnp.ones_like(values)], axis=1)
        mixed = jnp.dot(weights, values, preferred_element_type=F32)
        mixed = (mixed[:, :LANE] / mixed[:, LANE:]).astype(BF16)
        for h in range(4):
            cols = slice((g * 2 + h % 2) * LANE, (g * 2 + h % 2 + 1) * LANE)
            out_ref[h // 2, :, cols] = mixed[h * LANE : (h + 1) * LANE]


def attend(here, queries, own, other, start, later):
    rows = lambda j, *_: (j, 0)
    whole = lambda j, *_: (0, 0)
    return pl.pallas_call(
        attend_kernel,
        grid_spec=pltpu.PrefetchScalarGridSpec(
            num_scalar_prefetch=1,
            grid=(4,),
            in_specs=[
                pl.BlockSpec((LANE, 1024), rows),
                pl.BlockSpec((512, 512), whole),
                pl.BlockSpec((512, 512), whole),
                pl.BlockSpec((LANE, LANE), rows),
                LATER,
                LATER,
            ],
            out_specs=pl.BlockSpec((2, LANE, 512), lambda j, *_: (0, j, 0)),
            scratch_shapes=[pltpu.VMEM((1024, 512), BF16)],
        ),
        out_shape=array(2, 512, 512),
        compiler_params=BIG,
        name="attend",
    )(here, queries, own, other, start, *later)


def cut_heads(heads, later):
    def kernel(heads_ref, _, *out_refs):
        for i, ref in enumerate(out_refs):
            ref[...] = heads_ref[:, i * LANE : (i + 1) * LANE, :]

    return local(kernel, "cut_heads", [array(2, LANE, 512)] * 4, (heads, later), [VMEM, LATER])


def place_heads(here, parts):
    def kernel(here_ref, *refs):
        x, hi = here_ref[3], here_ref[4]
        for i, ref in enumerate(refs[:4]):
            pair = 2 * ((x + STEPS_X[i] + NX) % NX)
            for g in range(2):
                seq = pair + (hi if g == 0 else 1 - hi)
                for h in range(2):
                    dst = pl.ds(pl.multiple_of(seq * 512 + h * 256, 256), 256)
                    refs[4][:, dst] = ref[h, :, g * 256 : (g + 1) * 256]

    return local(kernel, "place_heads", array(LANE, 4096), (here, *parts), [SMEM] + [VMEM] * 4)


def add(a, b):
    return a.astype(F32) + b.astype(F32)


def sum_y(block):
    sent = [move(block[a, b], to_y(flip)) for flip, a, b in ((2, 0, 1), (1, 1, 0), (3, 1, 1))]
    return [*sent, block[0, 0]]


def add_parts(parts, later):
    def kernel(*refs):
        refs[-1][...] = total_of([ref[...] for ref in refs[:4]]).astype(BF16)

    operands = (*parts, *later)
    specs = [VMEM] * 4 + [LATER] * len(later)
    return local(kernel, "add_parts", array(NZ, LANE, 256), operands, specs)


def total_of(parts):
    total = parts[0].astype(F32)
    for part in parts[1:]:
        total = total + part.astype(F32)
    return total


def shards(tokens, norm_gain, query_weight, key_weight, value_weight, segment_ids, out_cotangent):
    blk, seq = lax.axis_index("blk"), lax.axis_index("seq")
    x, hi = seq // 2, seq % 2
    here = jnp.stack([blk // 4, (blk // 2) % 2, blk % 2, x, hi]).astype(jnp.int32)

    ring = ring_z(join_columns(key_weight, value_weight))
    column = stack_z(here, ring)
    near = [query_weight, *(move(query_weight, to_y(k)) for k in (2, 1, 3))]
    normed = normalize(here, tokens[0], norm_gain)
    wide = all_z_and_cores(pack_queries(near, (normed, ring[1], ring[2])))

    rows, _ = gather_x(normed, column)
    pieces = [column, *(move(column, to_y(k)) for k in (2, 1, 3))]
    other_pieces = [move(piece, to_core) for piece in pieces]

    chunks = 2 * ((x + jnp.array(STEPS_X, jnp.int32) + NX) % NX) + hi
    place_in = (chunks[:, None] * LANE + jnp.arange(LANE, dtype=jnp.int32)[None, :]).reshape(-1)
    half = HEAD_DIM // 2
    expo = jnp.arange(half, dtype=F32) * (2.0 / HEAD_DIM)
    freq = jnp.power(jnp.float32(500000.0), -expo)
    angle = place_in.astype(F32)[:, None] * freq[None, :]
    cosine, sine = jnp.cos(angle), jnp.sin(angle)
    cosine = jnp.concatenate([cosine, cosine], axis=1)
    sine = jnp.concatenate([-sine, sine], axis=1)
    segment = segment_ids[0]
    mine = jnp.concatenate([lax.dynamic_slice_in_dim(segment, chunks[i] * LANE, LANE) for i in range(4)])
    start = jnp.sum((segment[None, :] < mine[:, None]).astype(jnp.int32), axis=1)
    start = jnp.broadcast_to(start[:, None], (512, LANE))

    inputs, part = own_part(here, rows, pieces)
    own_kv = keys_values(here, inputs, part, other_pieces, cosine, sine, start)
    other_kv = move(own_kv, to_y(2))
    queries = project(inputs, wide, cosine, sine)
    cot_own, cot_other = order_cotangent(here, out_cotangent[0], rows[1:3])
    cot_other, _ = gather_x(cot_other, own_kv)
    cot_own, sent = gather_x(cot_own, queries)
    cot_other = stack_rows(cot_other, queries)
    heads = attend(here, queries, own_kv, other_kv, start, sent)
    cot_own = stack_rows(cot_own, queries)

    def product(columns, half):
        return lax.dot_general(columns, heads[half], (((0,), (0,)), ((), ())), preferred_element_type=F32)

    from_core = [move(product(cot_other, half).astype(BF16), to_core) for half in range(2)]
    first, second = (add(product(cot_own, half), from_core[half]).astype(BF16) for half in range(2))
    quarters = [(a, b) for a in range(2) for b in range(2)]
    second = lax.psum_scatter(
        second, "blk", scatter_dimension=0, tiled=True, axis_index_groups=Z_GROUPS
    )
    first = first.reshape(8, 2, LANE, 512)
    first = sum_y({(a, b): first[:, a, :, b * 256 : (b + 1) * 256] for a, b in quarters})
    chunks = cut_heads(heads, first[1])
    parts = [chunks[0], *(move(chunks[i], to_x(-step)) for i, step in ((2, -1), (1, 1), (3, 2)))]
    mixed = place_heads(here, parts)
    first = swap_z(add_parts(first, parts[1:]))
    left = jnp.sum(first.astype(F32), axis=0)
    second = sum_y({(a, b): second[a * LANE : (a + 1) * LANE, b * 256 : (b + 1) * 256] for a, b in quarters})
    return (mixed[None], jnp.concatenate([left, total_of(second)], axis=1))


def solution(mesh):
    return jax.shard_map(
        shards,
        mesh=mesh,
        in_specs=(
            P("blk", "seq", None),
            P(),
            P("blk", "seq"),
            P("blk", "seq"),
            P("blk", "seq"),
            P("blk", None),
            P("blk", "seq", None),
        ),
        out_specs=(P("blk", "seq", None), P("blk", "seq")),
        check_vma=False,
    )
```
